32 devices in a mesh: groups: 2 (over x), expert: 16 (over z, y, core).
Axes of the slice: x: 2, y: 2, z: 4, core: 2. Of those that a mesh axis runs over, the one named last changes fastest.
Arguments:
- activations: bfloat16 [64, 6144], P(('groups', 'expert')), parts along dimension 0, may hold values from -6 to 6
- out_grads: bfloat16 [64, 6144], P(('groups', 'expert')), parts along dimension 0, may hold values from -6 to 6
- expert_ids: int32 [64, 4], P(('groups', 'expert')), parts along dimension 0, may hold values from 0 to 15, all different within a row; in each aligned block of 2 rows (0 to 1, 2 to 3, ...) at most 2 rows name the same one
- route_scores: float32 [64, 4], P(('groups', 'expert')), parts along dimension 0, may hold values from 0.05 to 1
- w_gate: bfloat16 [43008, 6144], P('expert'), may hold values from -0.078125 to 0.078125
- w_up: bfloat16 [43008, 6144], P('expert'), may hold values from -0.078125 to 0.078125
Outputs:
- fisher: bfloat16 [86016, 6144], P(('groups', 'expert')), parts along dimension 0
The draws below stay inside these ranges and needn't reach their ends.
There are 2 independent parts, one for each index of `groups`. The reference program is written for one: setup_inputs(seed, part) draws one part's arguments, and reference() takes and returns one part's arrays. A program takes and returns all parts, laid end to end along the dimension named above; an argument that names none is the same for every part. Nothing has to cross between parts.
Inputs may be any that keep to these rules, and one draw needn't show every extreme that they name: `expert_ids`: each row names 4 different experts; every expert is named somewhere; in the rows of one device no expert is named by more than 2 rows, a bound that some block reaches.
All inputs are finite; a program needn't handle non-finite values.
Results may differ from the reference program's by a relative error of at most 0.0091.
Values may be sent and summed in bfloat16 or wider, within the bound.
A program may use at most 320 MiB of HBM per device.

```python
import math
import jax
import jax.numpy as jnp
import numpy as np
from jax import lax

D = 6144
FF = 10752
N_ALL = 16
TOP = 4
EXPERTS = 4
TOK_DEV = 2
TOKENS = 32
CAP = 2


def steps_of(rng, shape, cuts, least, top_value):
    gain, own = 1.0, jax.random.fold_in(rng, 6)
    for axis_at, shards_of in cuts:
        steps = jnp.exp(jax.random.uniform(jax.random.fold_in(own, axis_at), (shards_of,), jnp.float32, least / len(cuts), top_value / len(cuts)))
        gain = gain * jnp.repeat(steps, shape[axis_at] // shards_of).reshape([-1 if axis == axis_at else 1 for axis in range(len(shape))])
    return gain


def assign_block(stream_key, own, number, rows, number_of, top, bound, skew):
    sequence = jax.random.permutation(stream_key, number_of)
    crowded, usual = load_shares(number_of, rows * top, bound, skew, True), load_shares(number_of, rows * top, bound, skew, False)
    places = jnp.arange(number_of)

    def named(lengths, rotation):
        used = int((lengths > 0).sum())
        fixed = max(1, used // 4)
        shifted = fixed + (places - fixed + rotation * (used - fixed)) % max(1, number_of - fixed)
        return jnp.zeros((number_of,), jnp.int32).at[sequence[jnp.where(places < fixed, places, shifted)]].set(jnp.asarray(lengths, jnp.int32))

    lengths = jnp.where(number % 4 == 0, named(crowded, number // 4), named(usual, number - number // 4 - 1))
    mixed = jax.random.permutation(jax.random.fold_in(own, 3), number_of)
    giver, sink = mixed[0:number_of // 2 * 2:2], mixed[1:number_of // 2 * 2:2]
    room = jnp.minimum(lengths[giver] - 1, bound - lengths[sink]) // 2
    room = jnp.where((giver == sequence[0]) | (sink == sequence[0]) | (lengths[sink] == 0), 0, jnp.maximum(room, 0))
    shifted = jax.random.randint(jax.random.fold_in(own, 4), (number_of // 2,), 0, 1 << 20) % (room + 1)
    lengths = lengths.at[giver].add(-shifted).at[sink].add(shifted)
    labels = jnp.searchsorted(jnp.cumsum(lengths), jnp.arange(rows * top), side="right").astype(jnp.int32)
    grid = labels.reshape(top, rows).T
    grid = grid[jax.random.permutation(jax.random.fold_in(own, 1), rows)]
    rotation = jax.random.randint(jax.random.fold_in(own, 2), (rows, 1), 0, top)
    return jnp.take_along_axis(grid, (jnp.arange(top)[None, :] + rotation) % top, axis=1)


def load_shares(number_of, total, most, slope, full):
    loads = [(1 << 20) // math.isqrt(standing ** slope) + 1 for standing in range(1, number_of + 1)]
    largest = most if full else min(most, max(-(-total // number_of), total * loads[0] // sum(loads)))
    least = 1 if total - largest >= number_of - 1 else 0
    given, spare = [largest] + [least] * (number_of - 1), total - largest - least * (number_of - 1)
    while spare > 0:
        candidates = [i for i in range(1, number_of) if given[i] < largest] or [i for i in range(1, number_of) if given[i] < most]
        whole, remaining = sum([loads[i] for i in candidates]), spare
        for i in candidates:
            more = min(most - given[i], max(1, remaining * loads[i] // whole), spare)
            given[i] = given[i] + more
            spare = spare - more
    return np.array(given)


def normal_values(stream_key, extent, deviation, reach, cuts=(), kind=jnp.bfloat16):
    level = steps_of(stream_key, extent, cuts, -0.22, 0.18) if cuts else 1.0
    drawn = jax.random.normal(stream_key, extent, jnp.float32) * deviation * level
    return jnp.minimum(jnp.maximum(drawn, -reach), reach).astype(kind)


def setup_inputs(seed: int = 0, part: int = 0) -> dict:
    key_of = jax.random.split(jax.random.key(seed), 7)
    own_keys = jax.random.split(jax.random.fold_in(key_of[6], part), 7)
    activations = normal_values(own_keys[0], (TOKENS, D), 1.0, 6.0, ((0, 16),))
    out_grads = normal_values(own_keys[1], (TOKENS, D), 1.0, 6.0, ((0, 16),))
    expert_ids_keys = jax.random.split(jax.random.fold_in(own_keys[2], 1), TOKENS // TOK_DEV)
    expert_ids_turns = jax.random.permutation(jax.random.fold_in(own_keys[2], 3), TOKENS // TOK_DEV)
    expert_ids = jax.vmap(lambda own, number: assign_block(jax.random.fold_in(own_keys[2], 2), own, number, TOK_DEV, N_ALL, TOP, CAP, 2))(expert_ids_keys, expert_ids_turns).reshape((TOKENS, TOP))
    route_scores = jnp.clip(jnp.exp(math.log(1.0) - 2.9957323 * jax.random.uniform(own_keys[3], (TOKENS, TOP), jnp.float32) ** steps_of(own_keys[3], (TOKENS, TOP), ((0, 16),), -0.2, 0.2)), 0.05, 1.0)
    w_gate = normal_values(key_of[4], (EXPERTS * FF, D), D ** -0.5, 0.078125, ((0, 16),))
    w_up = normal_values(key_of[5], (EXPERTS * FF, D), D ** -0.5, 0.078125, ((0, 16),))
    return {"activations": activations, "out_grads": out_grads, "expert_ids": expert_ids, "route_scores": route_scores, "w_gate": w_gate, "w_up": w_up}


def fisher_term(rows, scaled, gate_rows, up_rows):
    dims = (((1,), (1,)), ((), ()))
    gate = lax.dot_general(rows, gate_rows, dims, preferred_element_type=jnp.float32)
    upper = lax.dot_general(rows, up_rows, dims, preferred_element_type=jnp.float32)
    hidden = jax.nn.silu(gate) * upper
    hidden_sq = (hidden * hidden).astype(jnp.bfloat16)
    grad32 = scaled.astype(jnp.float32)
    grad_sq = (grad32 * grad32).astype(jnp.bfloat16)
    return lax.dot_general(hidden_sq, grad_sq, (((0,), (0,)), ((), ())), preferred_element_type=jnp.float32)


def reference(activations, out_grads, expert_ids, route_scores, w_gate, w_up):
    share = route_scores / jnp.sum(route_scores, axis=1, keepdims=True)
    columns = jnp.arange(EXPERTS, dtype=jnp.int32)
    picked = (expert_ids[:, :, None] == columns[None, None, :]).astype(jnp.float32)
    weight = jnp.sum(picked * share[:, :, None], axis=1).astype(jnp.bfloat16)
    blocks = []
    for index in range(EXPERTS):
        scaled = (weight[:, index:index + 1].astype(jnp.float32) * out_grads.astype(jnp.float32)).astype(jnp.bfloat16)
        gate_rows = w_gate[index * FF:(index + 1) * FF]
        up_rows = w_up[index * FF:(index + 1) * FF]
        blocks.append(fisher_term(activations, scaled, gate_rows, up_rows))
    raw = jnp.concatenate(blocks, axis=0)
    total = jnp.sum(raw)
    return (raw * (EXPERTS * FF * D / total)).astype(jnp.bfloat16)
```

```python
import functools

import jax
import jax.numpy as jnp
from jax import lax
from jax.experimental import pallas as pl
from jax.experimental.pallas import tpu as pltpu
from jax.sharding import PartitionSpec as P

EXPERTS = 4
LANES = 128
MESH = pl.DeviceIdType.MESH
NT = (((1,), (1,)), ((), ()))


def chunk_of(rows, most):
    best = 16
    for size in range(16, most + 1, 16):
        if rows % size == 0:
            best = size
    return best


def hidden_kernel(
    devices, chunk, slots, first,
    gate_ref, up_ref, act_ref, grad_ref, ids_ref, score_ref,
    hsq_ref, gsq_ref, scale_ref,
    wbuf, stage, wide, abuf, gsend, gbuf, acts, sums, pbuf,
    wsem, a_send, a_recv, g_send, g_recv, p_send, p_recv,
):
    group = lax.axis_index("groups")
    me = lax.axis_index("expert")
    chips = devices // 2
    chip, core = me // 2, me % 2
    twin = chip * 2 + (1 - core)
    rows, width = gate_ref.shape
    chunks = rows // chunk
    segments = width // LANES
    tok_rows = act_ref.shape[0]
    tokens = devices * tok_rows
    block = tok_rows * segments

    def weights(index, slot):
        span = pl.ds(pl.multiple_of(index * chunk, chunk), chunk)
        return (
            pltpu.make_async_copy(gate_ref.at[span], wbuf.at[slot, pl.ds(0, chunk)], wsem.at[slot, 0]),
            pltpu.make_async_copy(up_ref.at[span], wbuf.at[slot, pl.ds(chunk, chunk)], wsem.at[slot, 1]),
        )

    def remote(src, dst, send, recv, to):
        return pltpu.make_async_remote_copy(
            src_ref=src, dst_ref=dst, send_sem=send, recv_sem=recv,
            device_id=(group, to), device_id_type=MESH,
        )

    def each(low, high, body):
        lax.fori_loop(low, high, lambda i, c: (body(i), c)[1], 0)

    def start_weights(i):
        for copy in weights(i, i):
            copy.start()

    each(0, slots, start_weights)

    barrier = pltpu.get_barrier_semaphore()

    def greet(k):
        pl.semaphore_signal(
            barrier, inc=1, device_id=(group, lax.rem(me + k, devices)), device_id_type=MESH
        )

    each(1, devices, greet)

    def to_rows(value):
        for seg in range(segments):
            stage[pl.ds(seg, tok_rows, stride=segments), :] = value[:, seg * LANES:(seg + 1) * LANES]
        return stage[...]

    abuf[me] = to_rows(act_ref[...].astype(jnp.float32)).astype(jnp.bfloat16)
    pl.semaphore_wait(barrier, devices - 1)

    def peer(k):
        return lax.rem(chip + k, chips) * 2 + core

    def act_copy(k):
        return remote(abuf.at[me], abuf.at[me], a_send.at[k], a_recv.at[me], peer(k))

    def act_forward(k):
        source = peer(k)
        return remote(abuf.at[source], abuf.at[source], a_send.at[chips + k], a_recv.at[source], twin)

    act_forward(0).start()
    each(1, chips, lambda k: act_copy(k).start())

    score = score_ref[...]
    share = score / jnp.sum(score, axis=1, keepdims=True)
    ids = ids_ref[...]
    grad = to_rows(grad_ref[...].astype(jnp.float32))
    row_token = lax.broadcasted_iota(jnp.int32, (block, 1), 0) // segments
    for index in range(EXPERTS):
        weight = jnp.sum(jnp.where(ids == index, share, 0.0), axis=1, keepdims=True)
        weight = weight.astype(jnp.bfloat16).astype(jnp.float32)
        spread = jnp.zeros((block, 1), jnp.float32)
        for token in range(tok_rows):
            spread = jnp.where(row_token == token, weight[token:token + 1, :], spread)
        scaled = (grad * spread).astype(jnp.bfloat16).astype(jnp.float32)
        gsend[index] = (scaled * scaled).astype(jnp.bfloat16)
    gbuf[me] = gsend[me // (devices // EXPERTS)]

    def grad_copy(k):
        to = peer(k)
        return remote(gsend.at[to // (devices // EXPERTS)], gbuf.at[me], g_send.at[k], g_recv.at[me], to)

    def grad_forward(k):
        source = peer(k)
        return remote(gbuf.at[source], gbuf.at[source], g_send.at[chips + k], g_recv.at[source], twin)

    def pass_on(copy, forward):
        def one(k):
            source = lax.rem(chip - k + chips, chips) * 2 + core
            remote(abuf.at[me], abuf.at[source], a_send.at[k], copy.at[source], twin).wait_recv()
            forward(lax.rem(chips - k, chips)).start()

        each(1, chips, one)

    def from_twin(recv):
        def one(k):
            source = k * 2 + (1 - core)
            remote(abuf.at[me], abuf.at[source], a_send.at[0], recv.at[source], twin).wait_recv()

        each(0, chips, one)

    pass_on(a_recv, act_forward)
    grad_forward(0).start()
    each(1, chips, lambda k: grad_copy(k).start())
    from_twin(a_recv)

    def to_tokens(source, target):
        wide[...] = source[...].astype(jnp.float32).reshape(devices * block, LANES)
        total = jnp.zeros((tokens, LANES), jnp.float32)
        for seg in range(segments):
            piece = wide[pl.ds(seg, tokens, stride=segments), :]
            target[:, seg * LANES:(seg + 1) * LANES] = piece.astype(jnp.bfloat16)
            total = total + piece
        return total

    to_tokens(abuf, acts)
    sums[...] = jnp.zeros_like(sums)

    def hidden(index):
        slot = lax.rem(index, slots)
        for copy in weights(index, slot):
            copy.wait()
        both = lax.dot_general(wbuf[slot], acts[...], NT, preferred_element_type=jnp.float32)

        @pl.when(index + slots < chunks)
        def _():
            for copy in weights(index + slots, slot):
                copy.start()

        gate, upper = both[:chunk], both[chunk:]
        value = gate / (1.0 + jnp.exp(-gate)) * upper
        square = (value * value).astype(jnp.bfloat16)
        hsq_ref[pl.ds(pl.multiple_of(index * chunk, chunk), chunk), :] = square
        sums[...] += jnp.sum(square.astype(jnp.float32), axis=0, keepdims=True)

    each(0, first, hidden)
    pass_on(g_recv, grad_forward)
    from_twin(g_recv)
    grad_sum = jnp.sum(to_tokens(gbuf, gsq_ref), axis=1, keepdims=True)
    each(first, chunks, hidden)

    same = lax.broadcasted_iota(jnp.int32, (tokens, tokens), 0) == lax.broadcasted_iota(
        jnp.int32, (tokens, tokens), 1
    )
    column = jnp.sum(jnp.where(same, sums[...], 0.0), axis=1, keepdims=True)
    part = jnp.sum(column * grad_sum, axis=0, keepdims=True)
    pbuf[me] = jnp.broadcast_to(part, (8, LANES))

    def part_copy(k):
        return remote(pbuf.at[me], pbuf.at[me], p_send.at[k], p_recv.at[me], lax.rem(me + k, devices))

    each(1, devices, lambda k: part_copy(k).start())

    def part_wait(k):
        source = lax.rem(me + k, devices)
        remote(pbuf.at[me], pbuf.at[source], p_send.at[k], p_recv.at[source], source).wait_recv()

    each(1, devices, part_wait)
    total = jnp.sum(pbuf[...], axis=0)
    scale_ref[...] = (float(devices) * rows * width) / total

    def drain(k):
        act_copy(k).wait_send()
        act_forward(k).wait_send()
        grad_copy(k).wait_send()
        grad_forward(k).wait_send()

    act_forward(0).wait_send()
    grad_forward(0).wait_send()
    each(1, chips, drain)
    each(1, devices, lambda k: part_copy(k).wait_send())


def outer_kernel(tile, hsq_ref, gsq_ref, scale_ref, out_ref):
    scale = scale_ref[0:1, 0:1]
    left = hsq_ref[...]
    for start in range(0, out_ref.shape[1], tile):
        span = slice(start, start + tile)
        raw = jnp.dot(left, gsq_ref[:, span], preferred_element_type=jnp.float32)
        out_ref[:, span] = (raw * scale).astype(jnp.bfloat16)


def per_device(activations, out_grads, expert_ids, route_scores, w_gate, w_up):
    devices = lax.axis_size("expert")
    rows, width = w_gate.shape
    tok_rows = activations.shape[0]
    tokens = devices * tok_rows
    segments = width // LANES
    block = tok_rows * segments
    chunk = chunk_of(rows, 128)
    chunks = rows // chunk
    slots = min(12, chunks)
    chips = devices // 2
    vmem = pl.BlockSpec(memory_space=pltpu.VMEM)
    anywhere = pl.BlockSpec(memory_space=pl.ANY)
    dma = pltpu.SemaphoreType.DMA
    bf16, f32 = jnp.bfloat16, jnp.float32
    hsq, gsq, scale = pl.pallas_call(
        functools.partial(hidden_kernel, devices, chunk, slots, chunks // 3),
        out_shape=(
            jax.ShapeDtypeStruct((rows, tokens), bf16),
            jax.ShapeDtypeStruct((tokens, width), bf16),
            jax.ShapeDtypeStruct((8, LANES), f32),
        ),
        in_specs=[anywhere, anywhere, vmem, vmem, vmem, vmem],
        out_specs=(vmem, vmem, vmem),
        scratch_shapes=[
            pltpu.VMEM((slots, 2 * chunk, width), bf16),
            pltpu.VMEM((block, LANES), f32),
            pltpu.VMEM((devices * block, LANES), f32),
            pltpu.VMEM((devices, block, LANES), bf16),
            pltpu.VMEM((EXPERTS, block, LANES), bf16),
            pltpu.VMEM((devices, block, LANES), bf16),
            pltpu.VMEM((tokens, width), bf16),
            pltpu.VMEM((1, tokens), f32),
            pltpu.VMEM((devices, 8, LANES), f32),
            dma((slots, 2)),
            dma((2 * chips,)),
            dma((devices,)),
            dma((2 * chips,)),
            dma((devices,)),
            dma((devices,)),
            dma((devices,)),
        ],
        compiler_params=pltpu.CompilerParams(
            collective_id=0, has_side_effects=True, vmem_limit_bytes=56 * 1024 * 1024
        ),
        cost_estimate=pl.CostEstimate(
            flops=4 * rows * width * tokens, bytes_accessed=4 * rows * width, transcendentals=rows * tokens
        ),
    )(w_gate, w_up, activations, out_grads, expert_ids, route_scores)

    height = chunk_of(rows, 256)
    return pl.pallas_call(
        functools.partial(outer_kernel, 512),
        out_shape=jax.ShapeDtypeStruct((rows, width), bf16),
        grid=(rows // height,),
        in_specs=[
            pl.BlockSpec((height, tokens), lambda i: (i, 0)),
            pl.BlockSpec((tokens, width), lambda i: (0, 0)),
            pl.BlockSpec((8, LANES), lambda i: (0, 0)),
        ],
        out_specs=pl.BlockSpec((height, width), lambda i: (i, 0)),
        compiler_params=pltpu.CompilerParams(vmem_limit_bytes=48 * 1024 * 1024),
        cost_estimate=pl.CostEstimate(
            flops=2 * rows * width * tokens, bytes_accessed=2 * rows * width, transcendentals=0
        ),
    )(hsq, gsq, scale)


def solution(mesh):
    return jax.shard_map(
        per_device,
        mesh=mesh,
        in_specs=(
            P(("groups", "expert"), None),
            P(("groups", "expert"), None),
            P(("groups", "expert"), None),
            P(("groups", "expert"), None),
            P("expert", None),
            P("expert", None),
        ),
        out_specs=P(("groups", "expert"), None),
        check_vma=False,
    )
```

```python
import functools

import jax
import jax.numpy as jnp
from jax import lax
from jax.experimental import pallas as pl
from jax.experimental.pallas import tpu as pltpu
from jax.sharding import PartitionSpec as P

EXPERTS = 4
LANES = 128
MESH = pl.DeviceIdType.MESH
NT = (((1,), (1,)), ((), ()))


def chunk_of(rows, most):
    best = 16
    for size in range(16, most + 1, 16):
        if rows % size == 0:
            best = size
    return best


def hidden_kernel(
    devices, chunk, slots, first,
    gate_ref, up_ref, act_ref, grad_ref, ids_ref, score_ref,
    hsq_ref, gsq_ref, scale_ref,
    wbuf, stage, wide, abuf, gsend, gbuf, acts, sums, pbuf,
    wsem, a_send, a_recv, g_send, g_recv, p_send, p_recv,
):
    group = lax.axis_index("groups")
    me = lax.axis_index("expert")
    chips = devices // 2
    chip, core = me // 2, me % 2
    twin = chip * 2 + (1 - core)
    rows, width = gate_ref.shape
    chunks = rows // chunk
    segments = width // LANES
    tok_rows = act_ref.shape[0]
    tokens = devices * tok_rows
    block = tok_rows * segments

    def weights(index, slot):
        span = pl.ds(pl.multiple_of(index * chunk, chunk), chunk)
        return (
            pltpu.make_async_copy(gate_ref.at[span], wbuf.at[slot, pl.ds(0, chunk)], wsem.at[slot, 0]),
            pltpu.make_async_copy(up_ref.at[span], wbuf.at[slot, pl.ds(chunk, chunk)], wsem.at[slot, 1]),
        )

    def remote(src, dst, send, recv, to):
        return pltpu.make_async_remote_copy(
            src_ref=src, dst_ref=dst, send_sem=send, recv_sem=recv,
            device_id=(group, to), device_id_type=MESH,
        )

    def each(low, high, body):
        lax.fori_loop(low, high, lambda i, c: (body(i), c)[1], 0)

    def start_weights(i):
        for copy in weights(i, i):
            copy.start()

    early, middle = min(2, slots), min(5, slots)
    each(0, early, start_weights)

    barrier = pltpu.get_barrier_semaphore()

    def greet(k):
        pl.semaphore_signal(
            barrier, inc=1, device_id=(group, lax.rem(me + k, devices)), device_id_type=MESH
        )

    each(1, devices, greet)

    def to_rows(value):
        for seg in range(segments):
            stage[pl.ds(seg, tok_rows, stride=segments), :] = value[:, seg * LANES:(seg + 1) * LANES]
        return stage[...]

    abuf[me] = to_rows(act_ref[...].astype(jnp.float32)).astype(jnp.bfloat16)
    pl.semaphore_wait(barrier, devices - 1)

    def peer(k):
        return lax.rem(chip + k, chips) * 2 + core

    def act_copy(k):
        return remote(abuf.at[me], abuf.at[me], a_send.at[k], a_recv.at[me], peer(k))

    def act_forward(k):
        source = peer(k)
        return remote(abuf.at[source], abuf.at[source], a_send.at[chips + k], a_recv.at[source], twin)

    act_forward(0).start()
    each(1, chips, lambda k: act_copy(k).start())

    score = score_ref[...]
    share = score / jnp.sum(score, axis=1, keepdims=True)
    ids = ids_ref[...]
    grad = to_rows(grad_ref[...].astype(jnp.float32))
    row_token = lax.broadcasted_iota(jnp.int32, (block, 1), 0) // segments
    for index in range(EXPERTS):
        weight = jnp.sum(jnp.where(ids == index, share, 0.0), axis=1, keepdims=True)
        weight = weight.astype(jnp.bfloat16).astype(jnp.float32)
        spread = jnp.zeros((block, 1), jnp.float32)
        for token in range(tok_rows):
            spread = jnp.where(row_token == token, weight[token:token + 1, :], spread)
        scaled = (grad * spread).astype(jnp.bfloat16).astype(jnp.float32)
        gsend[index] = (scaled * scaled).astype(jnp.bfloat16)
    gbuf[me] = gsend[me // (devices // EXPERTS)]

    def grad_copy(k):
        to = peer(k)
        return remote(gsend.at[to // (devices // EXPERTS)], gbuf.at[me], g_send.at[k], g_recv.at[me], to)

    def grad_forward(k):
        source = peer(k)
        return remote(gbuf.at[source], gbuf.at[source], g_send.at[chips + k], g_recv.at[source], twin)

    def pass_on(copy, forward):
        def one(k):
            source = lax.rem(chip - k + chips, chips) * 2 + core
            remote(abuf.at[me], abuf.at[source], a_send.at[k], copy.at[source], twin).wait_recv()
            forward(lax.rem(chips - k, chips)).start()

        each(1, chips, one)

    def from_twin(recv):
        def one(k):
            source = k * 2 + (1 - core)
            remote(abuf.at[me], abuf.at[source], a_send.at[0], recv.at[source], twin).wait_recv()

        each(0, chips, one)

    each(early, middle, start_weights)
    pass_on(a_recv, act_forward)
    each(middle, slots, start_weights)
    grad_forward(0).start()
    each(1, chips, lambda k: grad_copy(k).start())
    from_twin(a_recv)

    def to_tokens(source, target):
        wide[...] = source[...].astype(jnp.float32).reshape(devices * block, LANES)
        total = jnp.zeros((tokens, LANES), jnp.float32)
        for seg in range(segments):
            piece = wide[pl.ds(seg, tokens, stride=segments), :]
            target[:, seg * LANES:(seg + 1) * LANES] = piece.astype(jnp.bfloat16)
            total = total + piece
        return total

    to_tokens(abuf, acts)
    sums[...] = jnp.zeros_like(sums)

    def hidden(index):
        slot = lax.rem(index, slots)
        for copy in weights(index, slot):
            copy.wait()
        both = lax.dot_general(wbuf[slot], acts[...], NT, preferred_element_type=jnp.float32)

        @pl.when(index + slots < chunks)
        def _():
            for copy in weights(index + slots, slot):
                copy.start()

        gate, upper = both[:chunk], both[chunk:]
        value = gate / (1.0 + jnp.exp(-gate)) * upper
        square = (value * value).astype(jnp.bfloat16)
        hsq_ref[pl.ds(pl.multiple_of(index * chunk, chunk), chunk), :] = square
        sums[...] += jnp.sum(square.astype(jnp.float32), axis=0, keepdims=True)

    each(0, first, hidden)
    pass_on(g_recv, grad_forward)
    from_twin(g_recv)
    grad_sum = jnp.sum(to_tokens(gbuf, gsq_ref), axis=1, keepdims=True)
    each(first, chunks, hidden)

    same = lax.broadcasted_iota(jnp.int32, (tokens, tokens), 0) == lax.broadcasted_iota(
        jnp.int32, (tokens, tokens), 1
    )
    column = jnp.sum(jnp.where(same, sums[...], 0.0), axis=1, keepdims=True)
    part = jnp.sum(column * grad_sum, axis=0, keepdims=True)
    pbuf[me] = jnp.broadcast_to(part, (8, LANES))

    def part_copy(k):
        return remote(pbuf.at[me], pbuf.at[me], p_send.at[k], p_recv.at[me], lax.rem(me + k, devices))

    each(1, devices, lambda k: part_copy(k).start())

    def part_wait(k):
        source = lax.rem(me + k, devices)
        remote(pbuf.at[me], pbuf.at[source], p_send.at[k], p_recv.at[source], source).wait_recv()

    each(1, devices, part_wait)
    total = jnp.sum(pbuf[...], axis=0)
    scale_ref[...] = (float(devices) * rows * width) / total

    def drain(k):
        act_copy(k).wait_send()
        act_forward(k).wait_send()
        grad_copy(k).wait_send()
        grad_forward(k).wait_send()

    act_forward(0).wait_send()
    grad_forward(0).wait_send()
    each(1, chips, drain)
    each(1, devices, lambda k: part_copy(k).wait_send())


def outer_kernel(tile, hsq_ref, gsq_ref, scale_ref, out_ref):
    scale = scale_ref[0:1, 0:1]
    height = out_ref.shape[0]
    left = hsq_ref[pl.ds(pl.multiple_of(pl.program_id(0) * height, height), height), :]
    for start in range(0, out_ref.shape[1], tile):
        span = slice(start, start + tile)
        raw = jnp.dot(left, gsq_ref[:, span], preferred_element_type=jnp.float32)
        out_ref[:, span] = (raw * scale).astype(jnp.bfloat16)


def per_device(activations, out_grads, expert_ids, route_scores, w_gate, w_up):
    devices = lax.axis_size("expert")
    rows, width = w_gate.shape
    tok_rows = activations.shape[0]
    tokens = devices * tok_rows
    segments = width // LANES
    block = tok_rows * segments
    chunk = chunk_of(rows, 128)
    chunks = rows // chunk
    slots = min(10, chunks)
    chips = devices // 2
    vmem = pl.BlockSpec(memory_space=pltpu.VMEM)
    anywhere = pl.BlockSpec(memory_space=pl.ANY)
    dma = pltpu.SemaphoreType.DMA
    bf16, f32 = jnp.bfloat16, jnp.float32
    hsq, gsq, scale = pl.pallas_call(
        functools.partial(hidden_kernel, devices, chunk, slots, chunks // 3),
        out_shape=(
            jax.ShapeDtypeStruct((rows, tokens), bf16),
            jax.ShapeDtypeStruct((tokens, width), bf16),
            jax.ShapeDtypeStruct((8, LANES), f32),
        ),
        in_specs=[anywhere, anywhere, vmem, vmem, vmem, vmem],
        out_specs=(vmem, vmem, vmem),
        scratch_shapes=[
            pltpu.VMEM((slots, 2 * chunk, width), bf16),
            pltpu.VMEM((block, LANES), f32),
            pltpu.VMEM((devices * block, LANES), f32),
            pltpu.VMEM((devices, block, LANES), bf16),
            pltpu.VMEM((EXPERTS, block, LANES), bf16),
            pltpu.VMEM((devices, block, LANES), bf16),
            pltpu.VMEM((tokens, width), bf16),
            pltpu.VMEM((1, tokens), f32),
            pltpu.VMEM((devices, 8, LANES), f32),
            dma((slots, 2)),
            dma((2 * chips,)),
            dma((devices,)),
            dma((2 * chips,)),
            dma((devices,)),
            dma((devices,)),
            dma((devices,)),
        ],
        compiler_params=pltpu.CompilerParams(
            collective_id=0, has_side_effects=True, vmem_limit_bytes=44 * 1024 * 1024
        ),
        cost_estimate=pl.CostEstimate(
            flops=4 * rows * width * tokens, bytes_accessed=4 * rows * width, transcendentals=rows * tokens
        ),
    )(w_gate, w_up, activations, out_grads, expert_ids, route_scores)

    height = chunk_of(rows, 384)
    return pl.pallas_call(
        functools.partial(outer_kernel, 256),
        out_shape=jax.ShapeDtypeStruct((rows, width), bf16),
        grid=(rows // height,),
        in_specs=[
            vmem,
            vmem,
            vmem,
        ],
        out_specs=pl.BlockSpec((height, width), lambda i: (i, 0)),
        compiler_params=pltpu.CompilerParams(vmem_limit_bytes=20 * 1024 * 1024),
        cost_estimate=pl.CostEstimate(
            flops=2 * rows * width * tokens, bytes_accessed=2 * rows * width, transcendentals=0
        ),
    )(hsq, gsq, scale)


def solution(mesh):
    return jax.shard_map(
        per_device,
        mesh=mesh,
        in_specs=(
            P(("groups", "expert"), None),
            P(("groups", "expert"), None),
            P(("groups", "expert"), None),
            P(("groups", "expert"), None),
            P("expert", None),
            P("expert", None),
        ),
        out_specs=P(("groups", "expert"), None),
        check_vma=False,
    )
```

```python
import functools

import jax
import jax.numpy as jnp
from jax import lax
from jax.experimental import pallas as pl
from jax.experimental.pallas import tpu as pltpu
from jax.sharding import PartitionSpec as P

EXPERTS = 4
LANES = 128
MESH = pl.DeviceIdType.MESH
NT = (((1,), (1,)), ((), ()))


def chunk_of(rows, most):
    best = 16
    for size in range(16, most + 1, 16):
        if rows % size == 0:
            best = size
    return best


def hidden_kernel(
    devices, chunk, slots, first,
    gate_ref, up_ref, act_ref, grad_ref, ids_ref, score_ref,
    hsq_ref, gsq_ref, scale_ref,
    wbuf, stage, wide, abuf, gsend, gbuf, acts, sums, pbuf,
    wsem, a_send, a_recv, g_send, g_recv, p_send, p_recv,
):
    group = lax.axis_index("groups")
    me = lax.axis_index("expert")
    chips = devices // 2
    chip, core = me // 2, me % 2
    twin = chip * 2 + (1 - core)
    rows, width = gate_ref.shape
    chunks = rows // chunk
    segments = width // LANES
    tok_rows = act_ref.shape[0]
    tokens = devices * tok_rows
    block = tok_rows * segments

    def weights(index, slot):
        span = pl.ds(pl.multiple_of(index * chunk, chunk), chunk)
        return (
            pltpu.make_async_copy(gate_ref.at[span], wbuf.at[slot, pl.ds(0, chunk)], wsem.at[slot, 0]),
            pltpu.make_async_copy(up_ref.at[span], wbuf.at[slot, pl.ds(chunk, chunk)], wsem.at[slot, 1]),
        )

    def remote(src, dst, send, recv, to):
        return pltpu.make_async_remote_copy(
            src_ref=src, dst_ref=dst, send_sem=send, recv_sem=recv,
            device_id=(group, to), device_id_type=MESH,
        )

    def each(low, high, body):
        lax.fori_loop(low, high, lambda i, c: (body(i), c)[1], 0)

    def start_weights(i):
        for copy in weights(i, i):
            copy.start()

    early, middle = min(2, slots), min(4, slots)
    each(0, early, start_weights)

    barrier = pltpu.get_barrier_semaphore()

    def greet(k):
        pl.semaphore_signal(
            barrier, inc=1, device_id=(group, lax.rem(me + k, devices)), device_id_type=MESH
        )

    each(1, devices, greet)

    def to_rows(value):
        for seg in range(segments):
            stage[pl.ds(seg, tok_rows, stride=segments), :] = value[:, seg * LANES:(seg + 1) * LANES]
        return stage[...]

    abuf[me] = to_rows(act_ref[...].astype(jnp.float32)).astype(jnp.bfloat16)
    pl.semaphore_wait(barrier, devices - 1)

    def peer(k):
        return lax.rem(chip + k, chips) * 2 + core

    def act_copy(k):
        return remote(abuf.at[me], abuf.at[me], a_send.at[k], a_recv.at[me], peer(k))

    def act_forward(k):
        source = peer(k)
        return remote(abuf.at[source], abuf.at[source], a_send.at[chips + k], a_recv.at[source], twin)

    act_forward(0).start()
    each(1, chips, lambda k: act_copy(k).start())

    grad = to_rows(grad_ref[...].astype(jnp.float32))
    row_token = lax.broadcasted_iota(jnp.int32, (block, 1), 0) // segments

    def of_row(ref, k, zero):
        value = jnp.full((block, 1), zero)
        for token in range(tok_rows):
            value = jnp.where(row_token == token, ref[token, k], value)
        return value

    top = ids_ref.shape[1]
    ids = [of_row(ids_ref, k, jnp.int32(0)) for k in range(top)]
    score = [of_row(score_ref, k, jnp.float32(0)) for k in range(top)]
    whole = sum(score[1:], score[0])
    share = [value / whole for value in score]
    for index in range(EXPERTS):
        weight = sum(jnp.where(ids[k] == index, share[k], 0.0) for k in range(top))
        weight = weight.astype(jnp.bfloat16).astype(jnp.float32)
        scaled = (grad * weight).astype(jnp.bfloat16).astype(jnp.float32)
        gsend[index] = (scaled * scaled).astype(jnp.bfloat16)
    gbuf[me] = gsend[me // (devices // EXPERTS)]

    def grad_copy(k):
        to = peer(k)
        return remote(gsend.at[to // (devices // EXPERTS)], gbuf.at[me], g_send.at[k], g_recv.at[me], to)

    def grad_forward(k):
        source = peer(k)
        return remote(gbuf.at[source], gbuf.at[source], g_send.at[chips + k], g_recv.at[source], twin)

    def pass_on(copy, forward):
        def one(k):
            source = lax.rem(chip - k + chips, chips) * 2 + core
            remote(abuf.at[me], abuf.at[source], a_send.at[k], copy.at[source], twin).wait_recv()
            forward(lax.rem(chips - k, chips)).start()

        each(1, chips, one)

    def from_twin(recv):
        def one(k):
            source = k * 2 + (1 - core)
            remote(abuf.at[me], abuf.at[source], a_send.at[0], recv.at[source], twin).wait_recv()

        each(0, chips, one)

    each(early, middle, start_weights)
    pass_on(a_recv, act_forward)
    each(middle, slots, start_weights)
    grad_forward(0).start()
    each(1, chips, lambda k: grad_copy(k).start())
    from_twin(a_recv)

    def to_tokens(source, target):
        wide[...] = source[...].astype(jnp.float32).reshape(devices * block, LANES)
        total = jnp.zeros((tokens, LANES), jnp.float32)
        for seg in range(segments):
            piece = wide[pl.ds(seg, tokens, stride=segments), :]
            target[:, seg * LANES:(seg + 1) * LANES] = piece.astype(jnp.bfloat16)
            total = total + piece
        return total

    to_tokens(abuf, acts)
    sums[...] = jnp.zeros_like(sums)

    def hidden(index):
        slot = lax.rem(index, slots)
        for copy in weights(index, slot):
            copy.wait()
        both = lax.dot_general(wbuf[slot], acts[...], NT, preferred_element_type=jnp.float32)

        @pl.when(index + slots < chunks)
        def _():
            for copy in weights(index + slots, slot):
                copy.start()

        gate, upper = both[:chunk], both[chunk:]
        value = gate / (1.0 + jnp.exp(-gate)) * upper
        square = (value * value).astype(jnp.bfloat16)
        hsq_ref[pl.ds(pl.multiple_of(index * chunk, chunk), chunk), :] = square
        sums[...] += jnp.sum(square.astype(jnp.float32), axis=0, keepdims=True)

    each(0, first, hidden)
    pass_on(g_recv, grad_forward)
    from_twin(g_recv)
    grad_sum = jnp.sum(to_tokens(gbuf, gsq_ref), axis=1, keepdims=True)
    each(first, chunks, hidden)

    same = lax.broadcasted_iota(jnp.int32, (tokens, tokens), 0) == lax.broadcasted_iota(
        jnp.int32, (tokens, tokens), 1
    )
    column = jnp.sum(jnp.where(same, sums[...], 0.0), axis=1, keepdims=True)
    part = jnp.sum(column * grad_sum, axis=0, keepdims=True)
    pbuf[me] = jnp.broadcast_to(part, (8, LANES))

    def part_copy(k):
        return remote(pbuf.at[me], pbuf.at[me], p_send.at[k], p_recv.at[me], lax.rem(me + k, devices))

    each(1, devices, lambda k: part_copy(k).start())

    def part_wait(k):
        source = lax.rem(me + k, devices)
        remote(pbuf.at[me], pbuf.at[source], p_send.at[k], p_recv.at[source], source).wait_recv()

    each(1, devices, part_wait)
    total = jnp.sum(pbuf[...], axis=0)
    scale_ref[...] = (float(devices) * rows * width) / total

    def drain(k):
        act_copy(k).wait_send()
        act_forward(k).wait_send()
        grad_copy(k).wait_send()
        grad_forward(k).wait_send()

    act_forward(0).wait_send()
    grad_forward(0).wait_send()
    each(1, chips, drain)
    each(1, devices, lambda k: part_copy(k).wait_send())


def outer_kernel(tile, hsq_ref, gsq_ref, scale_ref, out_ref):
    scale = scale_ref[0:1, 0:1]
    height = out_ref.shape[0]
    left = hsq_ref[pl.ds(pl.multiple_of(pl.program_id(0) * height, height), height), :]
    for start in range(0, out_ref.shape[1], tile):
        span = slice(start, start + tile)
        raw = jnp.dot(left, gsq_ref[:, span], preferred_element_type=jnp.float32)
        out_ref[:, span] = (raw * scale).astype(jnp.bfloat16)


def per_device(activations, out_grads, expert_ids, route_scores, w_gate, w_up):
    devices = lax.axis_size("expert")
    rows, width = w_gate.shape
    tok_rows = activations.shape[0]
    tokens = devices * tok_rows
    segments = width // LANES
    block = tok_rows * segments
    chunk = chunk_of(rows, 192)
    chunks = rows // chunk
    slots = min(7, chunks)
    chips = devices // 2
    vmem = pl.BlockSpec(memory_space=pltpu.VMEM)
    anywhere = pl.BlockSpec(memory_space=pl.ANY)
    smem = pl.BlockSpec(memory_space=pltpu.SMEM)
    dma = pltpu.SemaphoreType.DMA
    bf16, f32 = jnp.bfloat16, jnp.float32
    hsq, gsq, scale = pl.pallas_call(
        functools.partial(hidden_kernel, devices, chunk, slots, chunks // 3),
        out_shape=(
            jax.ShapeDtypeStruct((rows, tokens), bf16),
            jax.ShapeDtypeStruct((tokens, width), bf16),
            jax.ShapeDtypeStruct((8, LANES), f32),
        ),
        in_specs=[anywhere, anywhere, vmem, vmem, smem, smem],
        out_specs=(vmem, vmem, vmem),
        scratch_shapes=[
            pltpu.VMEM((slots, 2 * chunk, width), bf16),
            pltpu.VMEM((block, LANES), f32),
            pltpu.VMEM((devices * block, LANES), f32),
            pltpu.VMEM((devices, block, LANES), bf16),
            pltpu.VMEM((EXPERTS, block, LANES), bf16),
            pltpu.VMEM((devices, block, LANES), bf16),
            pltpu.VMEM((tokens, width), bf16),
            pltpu.VMEM((1, tokens), f32),
            pltpu.VMEM((devices, 8, LANES), f32),
            dma((slots, 2)),
            dma((2 * chips,)),
            dma((devices,)),
            dma((2 * chips,)),
            dma((devices,)),
            dma((devices,)),
            dma((devices,)),
        ],
        compiler_params=pltpu.CompilerParams(
            collective_id=0, has_side_effects=True, vmem_limit_bytes=44 * 1024 * 1024
        ),
        cost_estimate=pl.CostEstimate(
            flops=4 * rows * width * tokens, bytes_accessed=4 * rows * width, transcendentals=rows * tokens
        ),
    )(w_gate, w_up, activations, out_grads, expert_ids, route_scores)

    height = chunk_of(rows, 384)
    return pl.pallas_call(
        functools.partial(outer_kernel, 256),
        out_shape=jax.ShapeDtypeStruct((rows, width), bf16),
        grid=(rows // height,),
        in_specs=[
            vmem,
            vmem,
            vmem,
        ],
        out_specs=pl.BlockSpec((height, width), lambda i: (i, 0)),
        compiler_params=pltpu.CompilerParams(vmem_limit_bytes=20 * 1024 * 1024),
        cost_estimate=pl.CostEstimate(
            flops=2 * rows * width * tokens, bytes_accessed=2 * rows * width, transcendentals=0
        ),
    )(hsq, gsq, scale)


def solution(mesh):
    return jax.shard_map(
        per_device,
        mesh=mesh,
        in_specs=(
            P(("groups", "expert"), None),
            P(("groups", "expert"), None),
            P(("groups", "expert"), None),
            P(("groups", "expert"), None),
            P("expert", None),
            P("expert", None),
        ),
        out_specs=P(("groups", "expert"), None),
        check_vma=False,
    )
```
